32 devices in a mesh: wide: 16 (over z, y, core), rep: 2 (over x).
Axes of the slice: x: 2, y: 2, z: 4, core: 2. Of those that a mesh axis runs over, the one named last changes fastest.
Arguments:
- features: bfloat16 [4096, 512], P(('wide', 'rep')), may hold values from -6 to 6
- w_query: bfloat16 [512, 512], replicated, may hold values from -0.25 to 0.25
- w_key: bfloat16 [512, 512], replicated, may hold values from -0.25 to 0.25
- w_out: bfloat16 [512, 512], replicated, may hold values from -0.25 to 0.25
- edge_weight: bfloat16 [16, 2, 6, 128, 128], P('wide', 'rep'), may hold values from -0.23925781 to 0.23925781
- tile_slot: int32 [16, 2, 6], P('wide', 'rep'), may hold values from 0 to 31, as said below
- tile_count: int32 [16, 2], P('wide', 'rep'), may hold values from 1 to 6, as said below
Outputs:
- updated: bfloat16 [4096, 512], P(('wide', 'rep'))
The draws below stay inside these ranges and needn't reach their ends.
Inputs may be any that keep to these rules, and one draw needn't show every extreme that they name: For each w and r the first tile_count[w, r] entries of tile_slot[w, r] are distinct and ascending; all 6 entries of a list are distinct. `tile_count`: some device has 6 live tiles.
All inputs are finite; a program needn't handle non-finite values.
Results may differ from the reference program's by a relative error of at most 0.014.
Values may be sent and summed in bfloat16 or wider, within the bound.
No kernel may reach another device: no remote copies, remote signals or barrier semaphores. Data moves between devices by JAX's collectives and lax.ppermute only.
A program may use at most 64 MiB of HBM per device.

```python
import jax
import jax.numpy as jnp
from jax import lax

F = 512
TILE = 128
N_NODES = 4096
TPD = 6
N_WIDE = 16
N_REP = 2


def tile_plan(key):
    base = jax.random.fold_in(key, 7)
    total_slots = N_WIDE * N_REP
    devices = N_WIDE * N_REP
    perm_keys = jax.random.split(jax.random.fold_in(base, 1), devices)
    perms = jax.vmap(lambda single: jax.random.permutation(single, total_slots)[:TPD])(perm_keys).astype(jnp.int32)
    levels = jax.random.randint(jax.random.fold_in(base, 2), (devices,), 0, 3).astype(jnp.int32)
    counts = jnp.maximum(TPD // jnp.left_shift(jnp.int32(1), levels), 1).astype(jnp.int32)
    busiest = jax.random.randint(jax.random.fold_in(base, 3), (), 0, devices)
    counts = jnp.where(jnp.arange(devices) == busiest, TPD, counts).astype(jnp.int32)
    order_key = jnp.where(jnp.arange(TPD)[None, :] < counts[:, None], perms, perms + total_slots)
    order = jnp.argsort(order_key, axis=1, stable=True)
    slots = jnp.take_along_axis(perms, order, axis=1)
    return (slots.reshape(N_WIDE, N_REP, TPD).astype(jnp.int32), counts.reshape(N_WIDE, N_REP))


def draw_tile_slot(key, part):
    return tile_plan(key)[0]


def draw_tile_count(key, part):
    return tile_plan(key)[1]


def steps_of(key, dims, cuts, smallest, largest):
    gain, own = 1.0, jax.random.fold_in(key, 6)
    for axis_at, parts in cuts:
        steps = jnp.exp(jax.random.uniform(jax.random.fold_in(own, axis_at), (parts,), jnp.float32, smallest / len(cuts), largest / len(cuts)))
        gain = gain * jnp.repeat(steps, dims[axis_at] // parts).reshape([-1 if axis == axis_at else 1 for axis in range(len(dims))])
    return gain


def normal_values(own_key, dims, scale, bound, shards=(), held_as=jnp.bfloat16):
    loudness = steps_of(own_key, dims, shards, -0.22, 0.18) if shards else 1.0
    drawn = jax.random.normal(own_key, dims, jnp.float32) * scale * loudness
    return jnp.minimum(jnp.maximum(drawn, -bound), bound).astype(held_as)


def setup_inputs(seed: int = 0) -> dict:
    keys = jax.random.split(jax.random.key(seed), 8)
    features = normal_values(keys[0], (N_NODES, F), 1.0, 6.0, ((0, 32),))
    w_query = normal_values(keys[1], (F, F), F ** -0.5, 0.25)
    w_key = normal_values(keys[2], (F, F), F ** -0.5, 0.25)
    w_out = normal_values(keys[3], (F, F), F ** -0.5, 0.25)
    edge_weight = normal_values(keys[4], (N_WIDE, N_REP, TPD, TILE, TILE), 0.04, 0.23925781, ((0, 16), (1, 2)))
    tile_slot = draw_tile_slot(jax.random.fold_in(keys[7], 71), 0)
    tile_count = draw_tile_count(jax.random.fold_in(keys[7], 71), 0)
    return {"features": features, "w_query": w_query, "w_key": w_key, "w_out": w_out, "edge_weight": edge_weight, "tile_slot": tile_slot, "tile_count": tile_count}


def reference(features, w_query, w_key, w_out, edge_weight, tile_slot, tile_count):
    node_count = features.shape[0]
    query_rows = jnp.dot(features, w_query, preferred_element_type=jnp.float32).astype(jnp.bfloat16)
    key_rows = jnp.dot(features, w_key, preferred_element_type=jnp.float32).astype(jnp.bfloat16)
    query_blocks = query_rows.reshape(N_WIDE * N_REP, TILE, F)
    key_blocks = key_rows.reshape(N_WIDE * N_REP, TILE, F)
    factor = 1.0 / math_sqrt(F)

    def per_device(partial_value, device_num):
        wide_pos = device_num // N_REP
        rep_pos = device_num % N_REP
        tile_slots = tile_slot[wide_pos, rep_pos]
        live_count = tile_count[wide_pos, rep_pos]
        weights = edge_weight[wide_pos, rep_pos].astype(jnp.float32)
        step_of = tile_slots // N_REP
        row_block = (wide_pos * N_REP + tile_slots % N_REP).astype(jnp.int32)
        col_block = ((wide_pos - step_of) % N_WIDE * N_REP + rep_pos).astype(jnp.int32)
        receiver = query_blocks[row_block].astype(jnp.float32)
        sender = key_blocks[col_block].astype(jnp.float32)
        scores = jnp.einsum('tif,tjf->tij', receiver, sender) * factor
        weighted = (jnp.tanh(scores) * weights).astype(jnp.bfloat16)
        weighted = lax.optimization_barrier(weighted).astype(jnp.float32)
        contrib = jnp.einsum('tij,tjf->tif', weighted, sender)
        active = (jnp.arange(TPD, dtype=jnp.int32) < live_count).astype(jnp.float32)
        contrib = contrib * active[:, None, None]
        return (partial_value.at[row_block].add(contrib), None)
    partial_value = jnp.zeros((N_WIDE * N_REP, TILE, F), jnp.float32)
    partial_value = lax.scan(per_device, partial_value, jnp.arange(N_WIDE * N_REP, dtype=jnp.int32))[0]
    message = partial_value.reshape(node_count, F).astype(jnp.bfloat16)
    mixed = features.astype(jnp.float32) + jnp.dot(message, w_out, preferred_element_type=jnp.float32)
    return mixed.astype(jnp.bfloat16)

def math_sqrt(value):
    return float(value) ** 0.5
```

```python
import jax
import jax.numpy as jnp
from jax import lax
from jax.experimental import pallas as pl
from jax.experimental.pallas import tpu as pltpu
from jax.sharding import PartitionSpec as P

NT = (((1,), (1,)), ((), ()))


def xor_pairs(n, k):
    return [(i, i ^ k) for i in range(n)]


def gather_blocks(block, n_wide):
    def send(value, k):
        return lax.ppermute(value, "wide", xor_pairs(n_wide, k))

    held = {0: block}
    for k in range(4, n_wide, 4):
        held[k] = send(block, k)
    for k in list(held):
        held[k ^ 2] = send(held[k], 2)
    for k in list(held):
        held[k ^ 1] = send(held[k], 1)
    return held


def tiles_kernel(order, n_wide, n_rep, factor, slot_ref, count_ref, weight_ref, query_ref, *rest):
    blocks = rest[: len(order)]
    own_ref, others_ref, total, first, number = rest[len(order) :]
    wide_pos = lax.axis_index("wide")
    rep_pos = lax.axis_index("rep")
    for k in range(n_wide):
        number[k] = 0
        first[k] = 0

    def note(tile, carry):
        step = slot_ref[tile] // n_rep
        k = wide_pos ^ lax.rem(wide_pos - step + n_wide, n_wide)
        seen = number[k]
        first[k] = jnp.where(seen == 0, tile, first[k])
        number[k] = seen + 1
        return carry

    lax.fori_loop(0, count_ref[0], note, 0)
    total[...] = jnp.zeros_like(total)
    for k, block_ref in zip(order, blocks):

        def one_tile(tile, carry, block_ref=block_ref):
            part = lax.rem(lax.rem(slot_ref[tile], n_rep) - rep_pos + n_rep, n_rep)
            block = block_ref[...]
            scores = lax.dot_general(query_ref[part], block, NT, preferred_element_type=jnp.float32)
            weighted = jnp.tanh(scores * factor) * weight_ref[tile].astype(jnp.float32)
            total[part] += jnp.dot(
                weighted.astype(jnp.bfloat16), block, preferred_element_type=jnp.float32
            )
            return carry

        lax.fori_loop(first[k], first[k] + number[k], one_tile, 0)
    own_ref[...] = total[0]
    for part in range(1, n_rep):
        others_ref[part - 1] = total[part].astype(jnp.bfloat16)


def output_kernel(own_ref, w_key_ref, w_out_ref, features_ref, *rest):
    *received, out_ref = rest
    mixed = own_ref[...]
    for ref in received:
        mixed += ref[...].astype(jnp.float32)
    message = jnp.dot(
        mixed.astype(jnp.bfloat16), w_key_ref[...], preferred_element_type=jnp.float32
    ).astype(jnp.bfloat16)
    updated = features_ref[...].astype(jnp.float32) + jnp.dot(
        message, w_out_ref[...], preferred_element_type=jnp.float32
    )
    out_ref[...] = updated.astype(jnp.bfloat16)


def on_device(features, w_query, w_key, w_out, edge_weight, tile_slot, tile_count):
    rows, width = features.shape
    n_wide = lax.axis_size("wide")
    n_rep = lax.axis_size("rep")
    vmem = pl.BlockSpec(memory_space=pltpu.VMEM)
    smem = pl.BlockSpec(memory_space=pltpu.SMEM)

    held = gather_blocks(features, n_wide)
    queries = []
    for part in range(n_rep):
        block = features
        if part:
            block = lax.ppermute(
                features, "rep", [((i + part) % n_rep, i) for i in range(n_rep)]
            )
        query = jnp.dot(block, w_query, preferred_element_type=jnp.float32).astype(jnp.bfloat16)
        query = lax.dot_general(query, w_key, NT, preferred_element_type=jnp.float32)
        queries.append(query.astype(jnp.bfloat16))
    order = list(held)
    own, others = pl.pallas_call(
        lambda *refs: tiles_kernel(order, n_wide, n_rep, 1.0 / float(width) ** 0.5, *refs),
        out_shape=(
            jax.ShapeDtypeStruct((rows, width), jnp.float32),
            jax.ShapeDtypeStruct((n_rep - 1, rows, width), jnp.bfloat16),
        ),
        in_specs=[smem, smem] + [vmem] * (2 + len(order)),
        out_specs=(vmem, vmem),
        scratch_shapes=[
            pltpu.VMEM((n_rep, rows, width), jnp.float32),
            pltpu.SMEM((n_wide,), jnp.int32),
            pltpu.SMEM((n_wide,), jnp.int32),
        ],
        compiler_params=pltpu.CompilerParams(vmem_limit_bytes=48 << 20),
        name="tiles",
    )(
        tile_slot[0, 0],
        tile_count[0],
        edge_weight[0, 0],
        jnp.stack(queries),
        *[held[k] for k in order],
    )
    received = [
        lax.ppermute(others[part - 1], "rep", [(i, (i + part) % n_rep) for i in range(n_rep)])
        for part in range(1, n_rep)
    ]
    return pl.pallas_call(
        output_kernel,
        out_shape=jax.ShapeDtypeStruct((rows, width), jnp.bfloat16),
        in_specs=[vmem] * (4 + len(received)),
        out_specs=vmem,
        compiler_params=pltpu.CompilerParams(vmem_limit_bytes=32 << 20),
        name="output",
    )(own, w_key, w_out, features, *received)


def solution(mesh):
    in_specs = (
        P(("wide", "rep"), None),
        P(),
        P(),
        P(),
        P("wide", "rep", None, None, None),
        P("wide", "rep", None),
        P("wide", "rep"),
    )
    out_specs = P(("wide", "rep"), None)
    return jax.shard_map(
        on_device, mesh=mesh, in_specs=in_specs, out_specs=out_specs, check_vma=False
    )
```

```python
import jax
import jax.numpy as jnp
from jax import lax
from jax.experimental import pallas as pl
from jax.experimental.pallas import tpu as pltpu
from jax.sharding import PartitionSpec as P

CORE, NEAR, FAR = 1, 2, 4
NT = (((1,), (1,)), ((), ()))
VMEM = pl.BlockSpec(memory_space=pltpu.VMEM)
SMEM = pl.BlockSpec(memory_space=pltpu.SMEM)
PARAMS = pltpu.CompilerParams(vmem_limit_bytes=40 << 20)


def send(value, k):
    return lax.ppermute(value, "wide", [(w, w ^ k) for w in range(lax.axis_size("wide"))])


def turn_rep(value, turn):
    n_rep = lax.axis_size("rep")
    return lax.ppermute(value, "rep", [(r, (r + turn) % n_rep) for r in range(n_rep)])


def cost(flops):
    return pl.CostEstimate(flops=flops, bytes_accessed=2 << 20, transcendentals=0)


def queries_kernel(n_rep, *refs):
    blocks, (w_query_ref, w_key_ref, query_ref) = refs[:n_rep], refs[n_rep:]
    for part, block_ref in enumerate(blocks):
        query = jnp.dot(
            block_ref[...], w_query_ref[...], preferred_element_type=jnp.float32
        ).astype(jnp.bfloat16)
        query_ref[part] = lax.dot_general(
            query, w_key_ref[...], NT, preferred_element_type=jnp.float32
        ).astype(jnp.bfloat16)


def note_tiles(n_wide, n_rep, list_ref, table_ref):
    wide_pos = lax.axis_index("wide")
    rep_pos = lax.axis_index("rep")
    for k in range(2 * n_wide):
        table_ref[k] = 0

    def note(tile, carry):
        slot = list_ref[1 + tile]
        step = slot // n_rep
        k = wide_pos ^ lax.rem(wide_pos - step + n_wide, n_wide)
        seen = table_ref[n_wide + k]
        table_ref[k] = jnp.where(seen == 0, tile, table_ref[k])
        table_ref[n_wide + k] = seen + 1
        table_ref[2 * n_wide + tile] = lax.rem(slot - step * n_rep - rep_pos + n_rep, n_rep)
        return carry

    lax.fori_loop(0, list_ref[0], note, 0)


def add_tiles(n_wide, factor, pieces, table_ref, weight_ref, query_ref, total, wanted):
    rows = weight_ref.shape[1]
    for block_ref, ks in pieces:
        for i, k in enumerate(ks):

            def one_tile(tile, carry, block_ref=block_ref, i=i):
                part = table_ref[2 * n_wide + tile]

                def work():
                    block = block_ref[i * rows : (i + 1) * rows, :]
                    scores = lax.dot_general(
                        query_ref[part], block, NT, preferred_element_type=jnp.float32
                    )
                    weighted = jnp.tanh(scores * factor) * weight_ref[tile].astype(jnp.float32)
                    total[part] += jnp.dot(
                        weighted.astype(jnp.bfloat16), block, preferred_element_type=jnp.float32
                    )

                if wanted == "all":
                    work()
                else:
                    pl.when((part == 0) if wanted == "own" else (part != 0))(work)
                return carry

            first = table_ref[k]
            lax.fori_loop(first, first + table_ref[n_wide + k], one_tile, 0)


def early_kernel(layout, n_wide, n_rep, factor, list_ref, weight_ref, query_ref, *rest):
    blocks, (total, table_ref) = rest[: len(layout)], rest[len(layout) :]
    note_tiles(n_wide, n_rep, list_ref, table_ref)
    total[...] = jnp.zeros_like(total)
    pieces = list(zip(blocks, layout))
    add_tiles(n_wide, factor, pieces, table_ref, weight_ref, query_ref, total, "all")


def others_kernel(layout, n_wide, n_rep, factor, list_ref, weight_ref, query_ref, early_ref, *rest):
    blocks, (out_ref, total, table_ref) = rest[: len(layout)], rest[len(layout) :]
    note_tiles(n_wide, n_rep, list_ref, table_ref)
    for part in range(1, n_rep):
        total[part] = early_ref[part]
    pieces = list(zip(blocks, layout))
    add_tiles(n_wide, factor, pieces, table_ref, weight_ref, query_ref, total, "others")
    for part in range(1, n_rep):
        out_ref[part - 1] = total[part].astype(jnp.bfloat16)


def own_kernel(layout, n_wide, n_rep, factor, list_ref, weight_ref, query_ref, early_ref, others_ref, w_key_ref, w_out_ref, features_ref, *rest):
    blocks, (out_ref, both_ref, total, table_ref) = rest[: len(layout)], rest[len(layout) :]
    note_tiles(n_wide, n_rep, list_ref, table_ref)
    total[0] = early_ref[0]
    pieces = list(zip(blocks, layout))
    add_tiles(n_wide, factor, pieces, table_ref, weight_ref, query_ref, total, "own")
    both_ref[...] = jnp.dot(
        w_key_ref[...], w_out_ref[...], preferred_element_type=jnp.float32
    ).astype(jnp.bfloat16)
    message = jnp.dot(
        total[0].astype(jnp.bfloat16), w_key_ref[...], preferred_element_type=jnp.float32
    ).astype(jnp.bfloat16)
    out_ref[...] = features_ref[...].astype(jnp.float32) + jnp.dot(
        message, w_out_ref[...], preferred_element_type=jnp.float32
    )


def output_kernel(own_ref, both_ref, *rest):
    *received, out_ref = rest
    mixed = received[0][...]
    if len(received) > 1:
        mixed = sum(ref[...].astype(jnp.float32) for ref in received).astype(jnp.bfloat16)
    updated = own_ref[...] + jnp.dot(mixed, both_ref[...], preferred_element_type=jnp.float32)
    out_ref[...] = updated.astype(jnp.bfloat16)


def on_device(features, w_query, w_key, w_out, edge_weight, tile_slot, tile_count):
    rows, width = features.shape
    n_wide = lax.axis_size("wide")
    n_rep = lax.axis_size("rep")
    factor = 1.0 / float(width) ** 0.5
    weights = edge_weight[0, 0]
    tile_list = jnp.concatenate([tile_count[0], tile_slot[0, 0]])

    held = {0: features, NEAR: send(features, NEAR)}
    relays = []
    far, bit = [0], n_wide // 2
    while bit >= FAR:
        for k in list(far):
            if k and not relays:
                relays = [turn_rep(features, -part) for part in range(1, n_rep)]
            held[k ^ bit] = send(held[k], bit)
            far.append(k ^ bit)
        bit //= 2
    top, end = n_wide // 2, n_wide - FAR
    for k in sorted(far)[1:]:
        value = held[k]
        if k == end:
            value = lax.optimization_barrier((value, held[FAR ^ NEAR], *relays))[0]
        held[k ^ NEAR] = send(value, NEAR)

    queries = pl.pallas_call(
        lambda *refs: queries_kernel(n_rep, *refs),
        out_shape=jax.ShapeDtypeStruct((n_rep, rows, width), jnp.bfloat16),
        in_specs=[VMEM] * (n_rep + 2),
        out_specs=VMEM,
        compiler_params=PARAMS,
        cost_estimate=cost(80 * n_rep * rows * width * width),
        name="queries",
    )(features, *relays, w_query, w_key)

    def other_core(ks):
        blocks = [held[k] for k in ks]
        both = jnp.concatenate(blocks, 0) if len(ks) > 1 else blocks[0]
        return send(both, CORE), [k ^ CORE for k in ks]

    groups = [[0, FAR, NEAR], [top, FAR ^ NEAR], [], [end ^ NEAR]]
    groups[2] = [k for k in held if not any(k in group for group in groups)]
    pairs = [other_core(group) for group in groups]
    soon = groups[0] + groups[1]
    early = [(held[k], [k]) for k in soon] + pairs[:2]
    late = [(held[k], [k]) for k in held if k not in soon] + pairs[2:]

    def call(kernel, pieces, inputs, out_shape, name, scratch=()):
        layout = [ks for _, ks in pieces]
        return pl.pallas_call(
            lambda *refs: kernel(layout, n_wide, n_rep, factor, *refs),
            out_shape=out_shape,
            in_specs=[SMEM] + [VMEM] * (1 + len(inputs) + len(pieces)),
            out_specs=jax.tree.map(lambda _: VMEM, out_shape),
            scratch_shapes=[*scratch, pltpu.SMEM((2 * n_wide + tile_slot.shape[-1],), jnp.int32)],
            compiler_params=PARAMS,
            cost_estimate=cost(240 * rows * rows * width),
            name=name,
        )(tile_list, weights, *inputs, *[block for block, _ in pieces])

    totals = jax.ShapeDtypeStruct((n_rep, rows, width), jnp.float32)
    total = call(early_kernel, early, [queries], totals, "early")
    others = call(
        others_kernel,
        late,
        [queries, total],
        jax.ShapeDtypeStruct((n_rep - 1, rows, width), jnp.bfloat16),
        "others",
        [pltpu.VMEM((n_rep, rows, width), jnp.float32)],
    )
    received = [turn_rep(others[part - 1], part) for part in range(1, n_rep)]
    own, both = call(
        own_kernel,
        late,
        [queries, total, others, w_key, w_out, features],
        (
            jax.ShapeDtypeStruct((rows, width), jnp.float32),
            jax.ShapeDtypeStruct(w_key.shape, jnp.bfloat16),
        ),
        "own",
        [pltpu.VMEM((1, rows, width), jnp.float32)],
    )
    return pl.pallas_call(
        output_kernel,
        out_shape=jax.ShapeDtypeStruct((rows, width), jnp.bfloat16),
        in_specs=[VMEM] * (2 + len(received)),
        out_specs=VMEM,
        compiler_params=PARAMS,
        name="output",
    )(own, both, *received)


def solution(mesh):
    in_specs = (
        P(("wide", "rep"), None),
        P(),
        P(),
        P(),
        P("wide", "rep", None, None, None),
        P("wide", "rep", None),
        P("wide", "rep"),
    )
    out_specs = P(("wide", "rep"), None)
    return jax.shard_map(
        on_device, mesh=mesh, in_specs=in_specs, out_specs=out_specs, check_vma=False
    )
```

```python
import jax
import jax.numpy as jnp
from jax import lax
from jax.experimental import pallas as pl
from jax.experimental.pallas import tpu as pltpu
from jax.sharding import PartitionSpec as P

CORE, NEAR, FAR = 1, 2, 4
NT = (((1,), (1,)), ((), ()))
VMEM = pl.BlockSpec(memory_space=pltpu.VMEM)
SMEM = pl.BlockSpec(memory_space=pltpu.SMEM)
PARAMS = pltpu.CompilerParams(vmem_limit_bytes=40 << 20)


def send(value, k):
    return lax.ppermute(value, "wide", [(w, w ^ k) for w in range(lax.axis_size("wide"))])


def turn_rep(value, turn):
    n_rep = lax.axis_size("rep")
    return lax.ppermute(value, "rep", [(r, (r + turn) % n_rep) for r in range(n_rep)])


def cost(flops):
    return pl.CostEstimate(flops=flops, bytes_accessed=2 << 20, transcendentals=0)


def queries_kernel(n_rep, *refs):
    blocks, (w_query_ref, w_key_ref, query_ref) = refs[:n_rep], refs[n_rep:]
    for part, block_ref in enumerate(blocks):
        query = jnp.dot(
            block_ref[...], w_query_ref[...], preferred_element_type=jnp.float32
        ).astype(jnp.bfloat16)
        query_ref[part] = lax.dot_general(
            query, w_key_ref[...], NT, preferred_element_type=jnp.float32
        ).astype(jnp.bfloat16)


def note_tiles(n_wide, n_rep, list_ref, table_ref):
    wide_pos = lax.axis_index("wide")
    rep_pos = lax.axis_index("rep")
    for k in range(2 * n_wide):
        table_ref[k] = 0

    def note(tile, carry):
        slot = list_ref[1 + tile]
        step = slot // n_rep
        k = wide_pos ^ lax.rem(wide_pos - step + n_wide, n_wide)
        seen = table_ref[n_wide + k]
        table_ref[k] = jnp.where(seen == 0, tile, table_ref[k])
        table_ref[n_wide + k] = seen + 1
        table_ref[2 * n_wide + tile] = lax.rem(slot - step * n_rep - rep_pos + n_rep, n_rep)
        return carry

    lax.fori_loop(0, list_ref[0], note, 0)


def add_tiles(n_wide, factor, pieces, table_ref, weight_ref, query_ref, total, wanted):
    rows = weight_ref.shape[1]
    for block_ref, ks in pieces:
        for i, k in enumerate(ks):

            def one_tile(tile, carry, block_ref=block_ref, i=i):
                part = table_ref[2 * n_wide + tile]
                at = 0 if wanted == "own" else part - 1

                @pl.when((part == 0) if wanted == "own" else (part != 0))
                def _():
                    block = block_ref[i * rows : (i + 1) * rows, :]
                    scores = lax.dot_general(
                        query_ref[part], block, NT, preferred_element_type=jnp.float32
                    )
                    weighted = jnp.tanh(scores * factor) * weight_ref[tile].astype(jnp.float32)
                    total[at] += jnp.dot(
                        weighted.astype(jnp.bfloat16), block, preferred_element_type=jnp.float32
                    )

                return carry

            first = table_ref[k]
            lax.fori_loop(first, first + table_ref[n_wide + k], one_tile, 0)


def early_kernel(layout, n_wide, n_rep, factor, list_ref, weight_ref, query_ref, *rest):
    blocks, (total, table_ref) = rest[: len(layout)], rest[len(layout) :]
    note_tiles(n_wide, n_rep, list_ref, table_ref)
    total[...] = jnp.zeros_like(total)
    pieces = list(zip(blocks, layout))
    add_tiles(n_wide, factor, pieces, table_ref, weight_ref, query_ref, total, "others")


def others_kernel(layout, n_wide, n_rep, factor, list_ref, weight_ref, query_ref, early_ref, *rest):
    blocks, (out_ref, total, table_ref) = rest[: len(layout)], rest[len(layout) :]
    note_tiles(n_wide, n_rep, list_ref, table_ref)
    total[...] = early_ref[...]
    pieces = list(zip(blocks, layout))
    add_tiles(n_wide, factor, pieces, table_ref, weight_ref, query_ref, total, "others")
    out_ref[...] = total[...].astype(jnp.bfloat16)


def own_kernel(layout, n_wide, n_rep, factor, list_ref, weight_ref, query_ref, others_ref, w_key_ref, w_out_ref, features_ref, *rest):
    blocks, (out_ref, both_ref, total, table_ref) = rest[: len(layout)], rest[len(layout) :]
    note_tiles(n_wide, n_rep, list_ref, table_ref)
    total[...] = jnp.zeros_like(total)
    pieces = list(zip(blocks, layout))
    add_tiles(n_wide, factor, pieces, table_ref, weight_ref, query_ref, total, "own")
    both_ref[...] = jnp.dot(
        w_key_ref[...], w_out_ref[...], preferred_element_type=jnp.float32
    ).astype(jnp.bfloat16)
    message = jnp.dot(
        total[0].astype(jnp.bfloat16), w_key_ref[...], preferred_element_type=jnp.float32
    ).astype(jnp.bfloat16)
    out_ref[...] = features_ref[...].astype(jnp.float32) + jnp.dot(
        message, w_out_ref[...], preferred_element_type=jnp.float32
    )


def output_kernel(own_ref, both_ref, *rest):
    *received, out_ref = rest
    mixed = received[0][...]
    if len(received) > 1:
        mixed = sum(ref[...].astype(jnp.float32) for ref in received).astype(jnp.bfloat16)
    updated = own_ref[...] + jnp.dot(mixed, both_ref[...], preferred_element_type=jnp.float32)
    out_ref[...] = updated.astype(jnp.bfloat16)


def on_device(features, w_query, w_key, w_out, edge_weight, tile_slot, tile_count):
    rows, width = features.shape
    n_wide = lax.axis_size("wide")
    n_rep = lax.axis_size("rep")
    factor = 1.0 / float(width) ** 0.5
    weights = edge_weight[0, 0]
    tile_list = jnp.concatenate([tile_count[0], tile_slot[0, 0]])

    held = {0: features, NEAR: send(features, NEAR)}
    relays = []
    far, bit = [0], n_wide // 2
    while bit >= FAR:
        for k in list(far):
            if k and not relays:
                relays = [turn_rep(features, -part) for part in range(1, n_rep)]
            held[k ^ bit] = send(held[k], bit)
            far.append(k ^ bit)
        bit //= 2
    top, end = n_wide // 2, n_wide - FAR
    for k in sorted(far)[1:]:
        value = held[k]
        if k == end:
            value = lax.optimization_barrier((value, *relays))[0]
        held[k ^ NEAR] = send(value, NEAR)

    queries = pl.pallas_call(
        lambda *refs: queries_kernel(n_rep, *refs),
        out_shape=jax.ShapeDtypeStruct((n_rep, rows, width), jnp.bfloat16),
        in_specs=[VMEM] * (n_rep + 2),
        out_specs=VMEM,
        compiler_params=PARAMS,
        cost_estimate=cost(80 * n_rep * rows * width * width),
        name="queries",
    )(features, *relays, w_query, w_key)

    def other_core(ks):
        blocks = [held[k] for k in ks]
        both = jnp.concatenate(blocks, 0) if len(ks) > 1 else blocks[0]
        return send(both, CORE), [k ^ CORE for k in ks]

    groups = [[0, FAR, NEAR], [top, FAR ^ NEAR], [], [end ^ NEAR]]
    groups[2] = [k for k in held if not any(k in group for group in groups)]
    pairs = [other_core(group) for group in groups]
    soon = [0, top, FAR, NEAR, FAR ^ NEAR, end]
    early = [(held[k], [k]) for k in soon] + pairs[:2]
    late = [(held[k], [k]) for k in held if k not in soon] + pairs[2:]

    def call(kernel, pieces, inputs, out_shape, name, scratch=()):
        layout = [ks for _, ks in pieces]
        return pl.pallas_call(
            lambda *refs: kernel(layout, n_wide, n_rep, factor, *refs),
            out_shape=out_shape,
            in_specs=[SMEM] + [VMEM] * (1 + len(inputs) + len(pieces)),
            out_specs=jax.tree.map(lambda _: VMEM, out_shape),
            scratch_shapes=[*scratch, pltpu.SMEM((2 * n_wide + tile_slot.shape[-1],), jnp.int32)],
            compiler_params=PARAMS,
            cost_estimate=cost(240 * rows * rows * width),
            name=name,
        )(tile_list, weights, *inputs, *[block for block, _ in pieces])

    totals = jax.ShapeDtypeStruct((n_rep - 1, rows, width), jnp.float32)
    total = call(early_kernel, early, [queries], totals, "early")
    others = call(
        others_kernel,
        late,
        [queries, total],
        jax.ShapeDtypeStruct((n_rep - 1, rows, width), jnp.bfloat16),
        "others",
        [pltpu.VMEM((n_rep - 1, rows, width), jnp.float32)],
    )
    received = [turn_rep(others[part - 1], part) for part in range(1, n_rep)]
    own, both = call(
        own_kernel,
        early + late,
        [queries, others, w_key, w_out, features],
        (
            jax.ShapeDtypeStruct((rows, width), jnp.float32),
            jax.ShapeDtypeStruct(w_key.shape, jnp.bfloat16),
        ),
        "own",
        [pltpu.VMEM((1, rows, width), jnp.float32)],
    )
    return pl.pallas_call(
        output_kernel,
        out_shape=jax.ShapeDtypeStruct((rows, width), jnp.bfloat16),
        in_specs=[VMEM] * (2 + len(received)),
        out_specs=VMEM,
        compiler_params=PARAMS,
        name="output",
    )(own, both, *received)


def solution(mesh):
    in_specs = (
        P(("wide", "rep"), None),
        P(),
        P(),
        P(),
        P("wide", "rep", None, None, None),
        P("wide", "rep", None),
        P("wide", "rep"),
    )
    out_specs = P(("wide", "rep"), None)
    return jax.shard_map(
        on_device, mesh=mesh, in_specs=in_specs, out_specs=out_specs, check_vma=False
    )
```

```python
import jax
import jax.numpy as jnp
from jax import lax
from jax.experimental import pallas as pl
from jax.experimental.pallas import tpu as pltpu
from jax.sharding import PartitionSpec as P

CORE, NEAR, FAR = 1, 2, 4
NT = (((1,), (1,)), ((), ()))
VMEM = pl.BlockSpec(memory_space=pltpu.VMEM)
SMEM = pl.BlockSpec(memory_space=pltpu.SMEM)
PARAMS = pltpu.CompilerParams(vmem_limit_bytes=40 << 20)


def send(value, k):
    return lax.ppermute(value, "wide", [(w, w ^ k) for w in range(lax.axis_size("wide"))])


def turn_rep(value, turn):
    n_rep = lax.axis_size("rep")
    return lax.ppermute(value, "rep", [(r, (r + turn) % n_rep) for r in range(n_rep)])


def cost(flops):
    return pl.CostEstimate(flops=flops, bytes_accessed=2 << 20, transcendentals=0)


def queries_kernel(n_rep, *refs):
    blocks, (w_query_ref, w_key_ref, query_ref) = refs[:n_rep], refs[n_rep:]
    for part, block_ref in enumerate(blocks):
        query = jnp.dot(
            block_ref[...], w_query_ref[...], preferred_element_type=jnp.float32
        ).astype(jnp.bfloat16)
        query_ref[part] = lax.dot_general(
            query, w_key_ref[...], NT, preferred_element_type=jnp.float32
        ).astype(jnp.bfloat16)


def note_tiles(n_wide, n_rep, list_ref, table_ref):
    wide_pos = lax.axis_index("wide")
    rep_pos = lax.axis_index("rep")
    for k in range(2 * n_wide):
        table_ref[k] = 0

    def note(tile, carry):
        slot = list_ref[1 + tile]
        step = slot // n_rep
        k = wide_pos ^ lax.rem(wide_pos - step + n_wide, n_wide)
        seen = table_ref[n_wide + k]
        table_ref[k] = jnp.where(seen == 0, tile, table_ref[k])
        table_ref[n_wide + k] = seen + 1
        table_ref[2 * n_wide + tile] = lax.rem(slot - step * n_rep - rep_pos + n_rep, n_rep)
        return carry

    lax.fori_loop(0, list_ref[0], note, 0)


def add_tiles(n_wide, factor, pieces, table_ref, weight_ref, query_ref, total, wanted):
    rows = weight_ref.shape[1]
    for block_ref, ks in pieces:
        for i, k in enumerate(ks):

            def one_tile(tile, carry, block_ref=block_ref, i=i):
                part = table_ref[2 * n_wide + tile]
                at = 0 if wanted == "own" else part - 1

                @pl.when((part == 0) if wanted == "own" else (part != 0))
                def _():
                    block = block_ref[i * rows : (i + 1) * rows, :]
                    scores = lax.dot_general(
                        query_ref[part], block, NT, preferred_element_type=jnp.float32
                    )
                    weighted = jnp.tanh(scores * factor) * weight_ref[tile].astype(jnp.float32)
                    total[at] += jnp.dot(
                        weighted.astype(jnp.bfloat16), block, preferred_element_type=jnp.float32
                    )

                return carry

            first = table_ref[k]
            lax.fori_loop(first, first + table_ref[n_wide + k], one_tile, 0)


def early_kernel(layout, n_wide, n_rep, factor, list_ref, weight_ref, query_ref, *rest):
    blocks, (total, table_ref) = rest[: len(layout)], rest[len(layout) :]
    note_tiles(n_wide, n_rep, list_ref, table_ref)
    total[...] = jnp.zeros_like(total)
    pieces = list(zip(blocks, layout))
    add_tiles(n_wide, factor, pieces, table_ref, weight_ref, query_ref, total, "others")


def others_kernel(layout, n_wide, n_rep, factor, list_ref, weight_ref, query_ref, early_ref, *rest):
    blocks, (out_ref, total, table_ref) = rest[: len(layout)], rest[len(layout) :]
    note_tiles(n_wide, n_rep, list_ref, table_ref)
    total[...] = early_ref[...]
    pieces = list(zip(blocks, layout))
    add_tiles(n_wide, factor, pieces, table_ref, weight_ref, query_ref, total, "others")
    out_ref[...] = total[...].astype(jnp.bfloat16)


def own_kernel(layout, n_wide, n_rep, factor, list_ref, weight_ref, query_ref, others_ref, w_key_ref, w_out_ref, features_ref, *rest):
    blocks, (out_ref, both_ref, total, table_ref) = rest[: len(layout)], rest[len(layout) :]
    note_tiles(n_wide, n_rep, list_ref, table_ref)
    total[...] = jnp.zeros_like(total)
    pieces = list(zip(blocks, layout))
    add_tiles(n_wide, factor, pieces, table_ref, weight_ref, query_ref, total, "own")
    both_ref[...] = jnp.dot(
        w_key_ref[...], w_out_ref[...], preferred_element_type=jnp.float32
    ).astype(jnp.bfloat16)
    message = jnp.dot(
        total[0].astype(jnp.bfloat16), w_key_ref[...], preferred_element_type=jnp.float32
    ).astype(jnp.bfloat16)
    out_ref[...] = features_ref[...].astype(jnp.float32) + jnp.dot(
        message, w_out_ref[...], preferred_element_type=jnp.float32
    )


def output_kernel(own_ref, both_ref, *rest):
    *received, out_ref = rest
    mixed = received[0][...]
    if len(received) > 1:
        mixed = sum(ref[...].astype(jnp.float32) for ref in received).astype(jnp.bfloat16)
    updated = own_ref[...] + jnp.dot(mixed, both_ref[...], preferred_element_type=jnp.float32)
    out_ref[...] = updated.astype(jnp.bfloat16)


def on_device(features, w_query, w_key, w_out, edge_weight, tile_slot, tile_count):
    rows, width = features.shape
    n_wide = lax.axis_size("wide")
    n_rep = lax.axis_size("rep")
    factor = 1.0 / float(width) ** 0.5
    weights = edge_weight[0, 0]
    tile_list = jnp.concatenate([tile_count[0], tile_slot[0, 0]])

    held = {0: features, NEAR: send(features, NEAR)}
    relays = []
    far, bit = [0], n_wide // 2
    while bit >= FAR:
        for k in list(far):
            if k and not relays:
                ready = lax.optimization_barrier((features, tile_list))[0]
                relays = [turn_rep(ready, -part) for part in range(1, n_rep)]
            held[k ^ bit] = send(held[k], bit)
            far.append(k ^ bit)
        bit //= 2
    top, end = n_wide // 2, n_wide - FAR
    for k in sorted(far)[1:]:
        value = held[k]
        if k == end:
            value = lax.optimization_barrier((value, *relays))[0]
        held[k ^ NEAR] = send(value, NEAR)

    queries = pl.pallas_call(
        lambda *refs: queries_kernel(n_rep, *refs),
        out_shape=jax.ShapeDtypeStruct((n_rep, rows, width), jnp.bfloat16),
        in_specs=[VMEM] * (n_rep + 2),
        out_specs=VMEM,
        compiler_params=PARAMS,
        cost_estimate=cost(80 * n_rep * rows * width * width),
        name="queries",
    )(features, *relays, w_query, w_key)

    def other_core(ks):
        blocks = [held[k] for k in ks]
        both = jnp.concatenate(blocks, 0) if len(ks) > 1 else blocks[0]
        return send(both, CORE), [k ^ CORE for k in ks]

    groups = [[0, FAR, NEAR], [top, FAR ^ NEAR], [], [end ^ NEAR]]
    groups[2] = [k for k in held if not any(k in group for group in groups)]
    pairs = [other_core(group) for group in groups]
    soon = [0, top, FAR, NEAR, FAR ^ NEAR, end]
    early = [(held[k], [k]) for k in soon] + pairs[:2]
    late = [(held[k], [k]) for k in held if k not in soon] + pairs[2:]

    def call(kernel, pieces, inputs, out_shape, name, scratch=()):
        layout = [ks for _, ks in pieces]
        return pl.pallas_call(
            lambda *refs: kernel(layout, n_wide, n_rep, factor, *refs),
            out_shape=out_shape,
            in_specs=[SMEM] + [VMEM] * (1 + len(inputs) + len(pieces)),
            out_specs=jax.tree.map(lambda _: VMEM, out_shape),
            scratch_shapes=[*scratch, pltpu.SMEM((2 * n_wide + tile_slot.shape[-1],), jnp.int32)],
            compiler_params=PARAMS,
            cost_estimate=cost(240 * rows * rows * width),
            name=name,
        )(tile_list, weights, *inputs, *[block for block, _ in pieces])

    totals = jax.ShapeDtypeStruct((n_rep - 1, rows, width), jnp.float32)
    total = call(early_kernel, early, [queries], totals, "early")
    others = call(
        others_kernel,
        late,
        [queries, total],
        jax.ShapeDtypeStruct((n_rep - 1, rows, width), jnp.bfloat16),
        "others",
        [pltpu.VMEM((n_rep - 1, rows, width), jnp.float32)],
    )
    received = [turn_rep(others[part - 1], part) for part in range(1, n_rep)]
    own, both = call(
        own_kernel,
        early + late,
        [queries, others, w_key, w_out, features],
        (
            jax.ShapeDtypeStruct((rows, width), jnp.float32),
            jax.ShapeDtypeStruct(w_key.shape, jnp.bfloat16),
        ),
        "own",
        [pltpu.VMEM((1, rows, width), jnp.float32)],
    )
    return pl.pallas_call(
        output_kernel,
        out_shape=jax.ShapeDtypeStruct((rows, width), jnp.bfloat16),
        in_specs=[VMEM] * (2 + len(received)),
        out_specs=VMEM,
        compiler_params=PARAMS,
        name="output",
    )(own, both, *received)


def solution(mesh):
    in_specs = (
        P(("wide", "rep"), None),
        P(),
        P(),
        P(),
        P("wide", "rep", None, None, None),
        P("wide", "rep", None),
        P("wide", "rep"),
    )
    out_specs = P(("wide", "rep"), None)
    return jax.shard_map(
        on_device, mesh=mesh, in_specs=in_specs, out_specs=out_specs, check_vma=False
    )
```
